512 devices in a mesh: outer: 16 (over y_hi, z), inner: 32 (over y_lo, x, core).
Axes of the slice: x: 4, y: 8 (y_hi: 2, y_lo: 4; y = y_hi * 4 + y_lo), z: 8, core: 2. Of those that a mesh axis runs over, the one named last changes fastest.
Arguments:
- queries: bfloat16 [65536, 32, 128], P(('outer', 'inner')), may hold values from -8 to 8
- key_states: bfloat16 [65536, 4, 128], P(('outer', 'inner')), may hold values from -8 to 8
- value_states: bfloat16 [65536, 4, 128], P(('outer', 'inner')), may hold values from -6 to 6
- out_grad: bfloat16 [65536, 32, 128], P(('outer', 'inner')), may hold values from -6 to 6
- bounds: int32 [3, 65536], P(None, ('outer', 'inner')), may hold values from 0 to 65535, as said below
Outputs:
- query_grad: bfloat16 [65536, 32, 128], P(('outer', 'inner'))
- key_grad: bfloat16 [65536, 4, 128], P(('outer', 'inner'))
- value_grad: bfloat16 [65536, 4, 128], P(('outer', 'inner'))
The draws below stay inside these ranges and needn't reach their ends.
Inputs may be any that keep to these rules, and one draw needn't show every extreme that they name: For each token t, bounds[0, t] is the first token of t's document (tokens of a document are consecutive), with t - 512 < bounds[0, t] <= t; in every draw some token has t - bounds[0, t] = 511. Either bounds[1, t] = bounds[2, t] = 0, or bounds[0, t] + 2 <= bounds[1, t] < bounds[2, t] <= t.
All inputs are finite; a program needn't handle non-finite values.
Results may differ from the reference program's by a relative error of at most 0.006.
Values may be sent and summed in bfloat16 or wider, within the bound.
A program may use at most 64 MiB of HBM per device.

```python
import math
import jax
import jax.numpy as jnp
from jax import lax

QH = 32
KVH = 4
HD = 128
TOK_DEV = 128
SPAN = 4
TOKENS = 65536


def doc_bounds(base_key):
    longest = SPAN * TOK_DEV
    shortest = max(longest // 8, 3)
    doc_count = TOKENS // shortest + 2
    parts = jax.random.split(base_key, 6)
    short_lengths = jax.random.randint(parts[0], (doc_count,), shortest, 2 * shortest + 1)
    long_lengths = jax.random.randint(parts[1], (doc_count,), longest // 2, longest + 1)
    pick_long = jax.random.randint(parts[2], (doc_count,), 0, 4) == 0
    lengths = jnp.where(pick_long, long_lengths, short_lengths).astype(jnp.int32)
    lead_length = jax.random.randint(parts[3], (), 1, TOK_DEV).astype(jnp.int32)
    lengths = lengths.at[0].set(lead_length).at[1].set(longest)
    doc_ends = jnp.cumsum(lengths).astype(jnp.int32)
    starts = doc_ends - lengths
    prompt_share = jax.random.randint(parts[4], (doc_count,), 2, 6)
    chosen_share = jax.random.randint(parts[5], (doc_count,), 2, 7)
    prompt = jnp.minimum(jnp.maximum(lengths * prompt_share // 8, 2), lengths)
    chosen = (lengths - prompt) * chosen_share // 8
    positions = jnp.arange(TOKENS, dtype=jnp.int32)
    doc_index = jnp.searchsorted(doc_ends, positions, side='right').astype(jnp.int32)
    doc_start = starts[doc_index]
    skip_low = doc_start + prompt[doc_index]
    skip_high = skip_low + chosen[doc_index]
    in_skip = (positions >= skip_high) & (skip_high > skip_low)
    low_edge = jnp.where(in_skip, skip_low, 0)
    high_edge = jnp.where(in_skip, skip_high, 0)
    frame = jnp.stack([doc_start, low_edge, high_edge]).astype(jnp.int32)
    return frame


def draw_bounds(key, part):
    frame = doc_bounds(jax.random.fold_in(key, 7))
    return frame


def draw_queries(key, part):
    values = jnp.clip(jax.random.normal(jax.random.fold_in(key, 21), (TOKENS, QH, HD), jnp.float32), -6.0, 6.0)
    return values.astype(jnp.bfloat16)


def draw_key_states(key, part):
    values = jnp.clip(jax.random.normal(jax.random.fold_in(key, 23), (TOKENS, KVH, HD), jnp.float32), -6.0, 6.0)
    return values.astype(jnp.bfloat16)


def block_levels(key, extent, pieces, least, largest):
    gain, own = 1.0, jax.random.fold_in(key, 6)
    for position, shards_of in pieces:
        heights = jnp.exp(jax.random.uniform(jax.random.fold_in(own, position), (shards_of,), jnp.float32, least / len(pieces), largest / len(pieces)))
        gain = gain * jnp.repeat(heights, extent[position] // shards_of).reshape([-1 if axis == position else 1 for axis in range(len(extent))])
    return gain


def gaussian(own_key, dims, scale, most, pieces=(), kind=jnp.bfloat16):
    entries = scale * jax.random.normal(own_key, dims, jnp.float32)
    if pieces:
        entries = entries * block_levels(own_key, dims, pieces, -0.22, 0.18)
    return jnp.clip(entries, -most, most).astype(kind)


def setup_inputs(seed: int = 0) -> dict:
    key_list = jax.random.split(jax.random.key(seed), 6)
    queries = draw_queries(jax.random.fold_in(key_list[5], 71), 0)
    key_states = draw_key_states(jax.random.fold_in(key_list[5], 71), 0)
    value_states = gaussian(key_list[2], (TOKENS, KVH, HD), 1.0, 6.0, ((0, 512),))
    out_grad = gaussian(key_list[3], (TOKENS, QH, HD), 1.0, 6.0, ((0, 512),))
    bounds = draw_bounds(jax.random.fold_in(key_list[5], 71), 0)
    return dict(queries=queries, key_states=key_states, value_states=value_states, out_grad=out_grad, bounds=bounds)


def visible(query_pos, key_pos, bounds):
    doc_start = bounds[0][:, None]
    skip_low = bounds[1][:, None]
    skip_high = bounds[2][:, None]
    key_row = key_pos[None, :]
    return (key_row >= doc_start) & (key_row <= query_pos[:, None]) & ((key_row < skip_low) | (key_row >= skip_high))


def reference(queries, key_states, value_states, out_grad, bounds):
    group_size = QH // KVH
    reach_rows = SPAN * TOK_DEV
    block_rows = math.gcd(512, TOKENS)
    score_scale = HD ** -0.5
    padded_keys = jnp.pad(key_states, ((reach_rows, 0), (0, 0), (0, 0)))
    padded_values = jnp.pad(value_states, ((reach_rows, 0), (0, 0), (0, 0)))
    query_four = queries.reshape(TOKENS, KVH, group_size, HD)
    grad_four = out_grad.reshape(TOKENS, KVH, group_size, HD)

    def scan_step(carried, block_index):
        key_sums, value_sums = carried
        first_row = block_index * block_rows
        query_block = lax.dynamic_slice_in_dim(query_four, first_row, block_rows, 0).astype(jnp.float32)
        grad_block = lax.dynamic_slice_in_dim(grad_four, first_row, block_rows, 0).astype(jnp.float32)
        key_block = lax.dynamic_slice_in_dim(padded_keys, first_row, block_rows + reach_rows, 0).astype(jnp.float32)
        value_block = lax.dynamic_slice_in_dim(padded_values, first_row, block_rows + reach_rows, 0).astype(jnp.float32)
        bound_block = lax.dynamic_slice_in_dim(bounds, first_row, block_rows, 1)
        query_pos = first_row + jnp.arange(block_rows, dtype=jnp.int32)
        key_pos = first_row - reach_rows + jnp.arange(block_rows + reach_rows, dtype=jnp.int32)
        seen_mask = visible(query_pos, key_pos, bound_block)
        scores = jnp.einsum("tkgd,skd->kgts", query_block, key_block) * score_scale
        grad_weights = jnp.einsum("tkgd,skd->kgts", grad_block, value_block)
        row_max = jnp.max(jnp.where(seen_mask, scores, -jnp.inf), axis=-1, keepdims=True)
        raw_weights = jnp.exp(jnp.where(seen_mask, scores - row_max, -jnp.inf))
        row_total = jnp.sum(raw_weights, axis=-1, keepdims=True)
        log_total = row_max + jnp.log(row_total)
        row_delta = jnp.sum(raw_weights * grad_weights, axis=-1, keepdims=True) / row_total
        prob = jnp.exp(jnp.where(seen_mask, scores - log_total, -jnp.inf))
        weights = lax.optimization_barrier(prob.astype(jnp.bfloat16)).astype(jnp.float32)
        dscore = lax.optimization_barrier((score_scale * prob * (grad_weights - row_delta)).astype(jnp.bfloat16)).astype(jnp.float32)
        query_part = jnp.einsum("kgts,skd->tkgd", dscore, key_block).reshape(block_rows, QH, HD).astype(jnp.bfloat16)
        key_part = jnp.einsum("kgts,tkgd->skd", dscore, query_block)
        value_part = jnp.einsum("kgts,tkgd->skd", weights, grad_block)
        key_sums = lax.dynamic_update_slice_in_dim(key_sums, lax.dynamic_slice_in_dim(key_sums, first_row, block_rows + reach_rows, 0) + key_part, first_row, 0)
        value_sums = lax.dynamic_update_slice_in_dim(value_sums, lax.dynamic_slice_in_dim(value_sums, first_row, block_rows + reach_rows, 0) + value_part, first_row, 0)
        return (key_sums, value_sums), query_part

    start_sums = jnp.zeros((TOKENS + reach_rows, KVH, HD), jnp.float32)
    (key_sums, value_sums), query_parts = lax.scan(scan_step, (start_sums, start_sums), jnp.arange(TOKENS // block_rows, dtype=jnp.int32))
    query_grad = query_parts.reshape(TOKENS, QH, HD)
    key_grad = key_sums[reach_rows:].astype(jnp.bfloat16)
    value_grad = value_sums[reach_rows:].astype(jnp.bfloat16)
    return (query_grad, key_grad, value_grad)
```

```python
import jax
import jax.numpy as jnp
from jax import lax
from jax.experimental import pallas as pl
from jax.experimental.pallas import tpu as pltpu
from jax.sharding import PartitionSpec as P

QH = 32
KVH = 4
HD = 128
SPAN = 4
GROUP = QH // KVH
MESH = pl.DeviceIdType.MESH
SCALE = HD**-0.5
SCALE2 = SCALE * 1.4426950408889634
HIDDEN = -1e30
F32 = jnp.float32
BF16 = jnp.bfloat16


def dot(a, b, dim_a, dim_b):
    return lax.dot_general(a, b, (((dim_a,), (dim_b,)), ((), ())), preferred_element_type=F32)


def make_kernel(devices, inner, rows, chunk):
    halo = SPAN * rows
    span = halo + rows
    band = halo + chunk

    def kernel(
        q_hbm, k_ref, v_ref, g_hbm, b_ref,
        dq_ref, dk_ref, dv_ref,
        q_in, g_in, q16, g16, kv, hide, acc, wide, dq32,
        to_near, to_other, near_in, other_in, far_out, far_in, own_out, own_in,
        in_sem, kv_send, kv_recv, pair_send, pair_recv, back_send, back_recv,
    ):
        me = lax.axis_index("outer") * inner + lax.axis_index("inner")
        odd = lax.rem(me, 2)
        even = odd == 0
        partner = me + 1 - 2 * odd

        def at(index):
            return (index // inner, lax.rem(index, inner))

        q_copy = pltpu.make_async_copy(q_hbm, q_in, in_sem.at[0])
        g_copy = pltpu.make_async_copy(g_hbm, g_in, in_sem.at[1])
        q_copy.start()
        g_copy.start()

        has_before = me >= 2
        has_after = me + 2 < devices

        for part, ref in ((0, k_ref), (1, v_ref)):
            wide[part] = ref[...].astype(F32)
            for c in range(KVH):
                own = wide[part, pl.ds(c, rows, stride=KVH), :]
                kv[c, part, pl.ds(halo, rows), :] = own.astype(BF16)

        @pl.when(me < SPAN)
        def _():
            kv[:, :, pl.ds(0, halo), :] = jnp.zeros((KVH, 2, halo, HD), BF16)

        @pl.when(jnp.logical_not(has_after))
        def _():
            far_in[...] = jnp.zeros(far_in.shape, BF16)
            own_in[...] = jnp.zeros(own_in.shape, BF16)

        barrier = pltpu.get_barrier_semaphore()

        @pl.when(has_before)
        def _():
            pl.semaphore_signal(barrier, inc=1, device_id=at(me - 2), device_id_type=MESH)

        @pl.when(odd == 1)
        def _():
            pl.semaphore_signal(barrier, inc=1, device_id=at(partner), device_id_type=MESH)

        waits = (1 - odd) + has_after.astype(jnp.int32)

        @pl.when(waits > 0)
        def _():
            pl.semaphore_wait(barrier, waits)

        def block(c, offset):
            start = (SPAN - offset) * rows
            if not isinstance(start, int):
                start = pl.multiple_of(start, rows)
            return kv.at[c, :, pl.ds(start, rows), :]

        def ahead(c, offset):
            kind = offset // 2
            return pltpu.make_async_remote_copy(
                block(c, offset), block(c, offset + 2), kv_send.at[kind, c], kv_recv.at[kind, c],
                device_id=at(me + 2), device_id_type=MESH,
            )

        def across(c, offset):
            kind = 2 + offset // 2
            return pltpu.make_async_remote_copy(
                block(c, offset - 1 + 2 * odd), block(c, offset), kv_send.at[kind, c],
                kv_recv.at[kind, c], device_id=at(partner), device_id_type=MESH,
            )

        def own_ahead(c):
            @pl.when(has_after)
            def _():
                ahead(c, 0).start()

        def relay(c):
            @pl.when(odd == 1)
            def _():
                across(c, 1).wait_recv()

            @pl.when(has_before)
            def _():
                ahead(c, 0).wait_recv()

                @pl.when(has_after)
                def _():
                    ahead(c, 2).start()

                @pl.when(even)
                def _():
                    across(c, 3).start()

                @pl.when(odd == 1)
                def _():
                    across(c, 1).start()

        def relay_last(c):
            @pl.when(me >= 4)
            def _():
                ahead(c, 2).wait_recv()

                @pl.when(odd == 1)
                def _():
                    across(c, 3).start()

        def all_here(c):
            @pl.when(even & has_before)
            def _():
                across(c, 1).wait_recv()

            @pl.when((me >= 4) | (me == 3))
            def _():
                across(c, 3).wait_recv()

        own_ahead(0)
        own_ahead(1)

        @pl.when(even)
        def _():
            for c in range(KVH):
                across(c, 1).start()

        base = (me - SPAN) * rows
        pos = lax.broadcasted_iota(jnp.int32, (span, rows), 0) + base
        query = lax.broadcasted_iota(jnp.int32, (span, rows), 1) + (base + halo)
        seen = (
            (pos >= b_ref[0:1, :])
            & (pos <= query)
            & ((pos < b_ref[1:2, :]) | (pos >= b_ref[2:3, :]))
        )
        hide[...] = jnp.where(seen, 0.0, HIDDEN).astype(BF16)

        def arrange(copy, source, target):
            copy.wait()
            for half in range(QH // 16):
                x = source[:, pl.ds(16 * half, 16), :].astype(F32)
                for k in range(16 // GROUP):
                    y = x[:, GROUP * k : GROUP * (k + 1), :].reshape(rows * GROUP, HD)
                    target[half * (16 // GROUP) + k] = y.astype(BF16)

        arrange(q_copy, q_in, q16)
        arrange(g_copy, g_in, g16)

        def compute(c, j):
            many = chunk * GROUP
            first = j * chunk
            key = kv[c, 0, pl.ds(first, band), :]
            value = kv[c, 1, pl.ds(first, band), :]
            queries = q16[c, pl.ds(first * GROUP, many), :]
            grads = g16[c, pl.ds(first * GROUP, many), :]
            lane = lax.broadcasted_iota(jnp.int32, (many, rows), 1)
            token = lax.broadcasted_iota(jnp.int32, (many, rows), 0) // GROUP + first
            mine = (lane == token).astype(BF16)
            scores = dot(
                jnp.concatenate([key, hide[pl.ds(first, band), :]], axis=1),
                jnp.concatenate([queries, mine], axis=1),
                1, 1,
            )
            grad_weights = dot(value, grads, 1, 1)
            top = jnp.max(scores, axis=0, keepdims=True)
            raw = jnp.exp2(scores * SCALE2 - top * SCALE2)
            total = jnp.sum(raw, axis=0, keepdims=True)
            weighted = jnp.sum(raw * grad_weights, axis=0, keepdims=True)
            inverse = 1.0 / total
            prob = raw * inverse
            dscore = (prob * (grad_weights - weighted * inverse)).astype(BF16)
            weights = prob.astype(BF16)
            for part, left, right in ((0, dscore, queries), (1, weights, grads)):
                add = dot(left, right, 1, 0)
                if j == 0:
                    acc[c, part, pl.ds(0, band), :] = add
                    acc[c, part, pl.ds(band, span - band), :] = jnp.zeros((span - band, HD), F32)
                else:
                    acc[c, part, pl.ds(first, band), :] += add
            query_part = dot(dscore, key, 0, 0) * SCALE
            dq32[pl.ds(first, chunk), pl.ds(GROUP * c, GROUP), :] = query_part.reshape(
                chunk, GROUP, HD
            )

        def pair(c, kind, source, target):
            return pltpu.make_async_remote_copy(
                source.at[c], target.at[c], pair_send.at[kind, c], pair_recv.at[kind, c],
                device_id=at(partner), device_id_type=MESH,
            )

        def back(c, kind, source, target):
            return pltpu.make_async_remote_copy(
                source.at[c], target.at[c], back_send.at[kind, c], back_recv.at[kind, c],
                device_id=at(me - 2), device_id_type=MESH,
            )

        odd_f = odd.astype(F32)

        def send_pair(c):
            near = pl.multiple_of(halo - rows - 2 * rows * odd, rows)
            other = pl.multiple_of(rows + 2 * rows * odd, rows)
            to_other[c] = acc[c, :, pl.ds(other, rows), :].astype(BF16)
            pair(c, 0, to_other, other_in).start()
            to_near[c] = acc[c, :, pl.ds(near, rows), :].astype(BF16)
            pair(c, 1, to_near, near_in).start()

        def send_far(c):
            pair(c, 0, to_other, other_in).wait_recv()
            far = acc[c, :, pl.ds(0, rows), :] + odd_f * other_in[c].astype(F32)
            far_out[c] = far.astype(BF16)

            @pl.when(has_before)
            def _():
                back(c, 0, far_out, far_in).start()

        def send_own(c):
            pair(c, 1, to_near, near_in).wait_recv()

            @pl.when(has_after)
            def _():
                back(c, 0, far_out, far_in).wait_recv()

            near = acc[c, :, pl.ds(2 * rows, rows), :] + near_in[c].astype(F32)
            own_out[c] = (near + far_in[c].astype(F32)).astype(BF16)

            @pl.when(has_before)
            def _():
                back(c, 1, own_out, own_in).start()

        def finish(c):
            @pl.when(has_after)
            def _():
                back(c, 1, own_out, own_in).wait_recv()

            own = acc[c, :, pl.ds(halo, rows), :] + (1.0 - odd_f) * other_in[c].astype(F32)
            own = own + own_in[c].astype(F32)
            wide[0, pl.ds(c, rows, stride=KVH), :] = own[0] * SCALE
            wide[1, pl.ds(c, rows, stride=KVH), :] = own[1]

        relay(0)
        own_ahead(2)
        relay_last(0)
        relay(1)
        own_ahead(3)
        for c in range(KVH):
            if c + 2 < KVH:
                relay(c + 2)
            if c + 1 < KVH:
                relay_last(c + 1)
            all_here(c)
            for j in range(rows // chunk):
                compute(c, j)
            send_pair(c)
            if c >= 1:
                send_far(c - 1)
            if c >= 2:
                send_own(c - 2)
            if c % 2 == 1:
                pick = pl.ds(GROUP * (c - 1), 2 * GROUP)
                dq_ref[:, pick, :] = dq32[:, pick, :].astype(BF16)
        send_far(KVH - 1)
        send_own(KVH - 2)
        finish(0)
        finish(1)
        send_own(KVH - 1)
        finish(2)
        finish(3)
        dk_ref[...] = wide[0].astype(BF16)
        dv_ref[...] = wide[1].astype(BF16)

        for c in range(KVH):
            pair(c, 0, to_other, other_in).wait_send()
            pair(c, 1, to_near, near_in).wait_send()

            @pl.when(has_before)
            def _():
                back(c, 0, far_out, far_in).wait_send()
                back(c, 1, own_out, own_in).wait_send()

            @pl.when(has_after)
            def _():
                ahead(c, 0).wait_send()

                @pl.when(has_before)
                def _():
                    ahead(c, 2).wait_send()

            @pl.when(even | has_before)
            def _():
                across(c, 1).wait_send()

            @pl.when((even & has_before) | (me >= 4))
            def _():
                across(c, 3).wait_send()

    return kernel


def solution(mesh):
    outer, inner = mesh.shape["outer"], mesh.shape["inner"]
    devices = outer * inner

    def per_device(queries, key_states, value_states, out_grad, bounds):
        rows = queries.shape[0]
        chunk = min(64, rows // 2)
        span = (SPAN + 1) * rows
        piece = pltpu.VMEM((KVH, 2, rows, HD), BF16)
        vmem = pl.BlockSpec(memory_space=pltpu.VMEM)
        anywhere = pl.BlockSpec(memory_space=pl.ANY)
        flat = (rows * KVH, HD)
        query_grad, key_grad, value_grad = pl.pallas_call(
            make_kernel(devices, inner, rows, chunk),
            out_shape=[
                jax.ShapeDtypeStruct((rows, QH, HD), BF16),
                jax.ShapeDtypeStruct(flat, BF16),
                jax.ShapeDtypeStruct(flat, BF16),
            ],
            in_specs=[anywhere, vmem, vmem, anywhere, vmem],
            out_specs=[vmem, vmem, vmem],
            scratch_shapes=[
                pltpu.VMEM((rows, QH, HD), BF16),
                pltpu.VMEM((rows, QH, HD), BF16),
                pltpu.VMEM((KVH, rows * GROUP, HD), BF16),
                pltpu.VMEM((KVH, rows * GROUP, HD), BF16),
                pltpu.VMEM((KVH, 2, span, HD), BF16),
                pltpu.VMEM((span, rows), BF16),
                pltpu.VMEM((KVH, 2, span, HD), F32),
                pltpu.VMEM((2, rows * KVH, HD), F32),
                pltpu.VMEM((rows, QH, HD), F32),
                piece, piece, piece, piece, piece, piece, piece, piece,
                pltpu.SemaphoreType.DMA((2,)),
                pltpu.SemaphoreType.DMA((4, KVH)),
                pltpu.SemaphoreType.DMA((4, KVH)),
                pltpu.SemaphoreType.DMA((2, KVH)),
                pltpu.SemaphoreType.DMA((2, KVH)),
                pltpu.SemaphoreType.DMA((2, KVH)),
                pltpu.SemaphoreType.DMA((2, KVH)),
            ],
            compiler_params=pltpu.CompilerParams(
                collective_id=0, has_side_effects=True, vmem_limit_bytes=48 * 2**20
            ),
            cost_estimate=pl.CostEstimate(
                flops=10 * QH * rows * span * HD,
                bytes_accessed=8 * rows * (QH + KVH) * HD,
                transcendentals=QH * rows * span,
            ),
        )(
            queries, key_states.reshape(flat), value_states.reshape(flat), out_grad, bounds
        )
        back = key_states.shape
        return query_grad, key_grad.reshape(back), value_grad.reshape(back)

    split = ("outer", "inner")
    whole = P(split, None, None)
    return jax.shard_map(
        per_device,
        mesh=mesh,
        in_specs=(whole, whole, whole, whole, P(None, split)),
        out_specs=(whole, whole, whole),
        check_vma=False,
    )
```

```python
import jax
import jax.numpy as jnp
from jax import lax
from jax.experimental import pallas as pl
from jax.experimental.pallas import tpu as pltpu
from jax.sharding import PartitionSpec as P

QH = 32
KVH = 4
HD = 128
SPAN = 4
GROUP = QH // KVH
MESH = pl.DeviceIdType.MESH
SCALE = HD**-0.5
SCALE2 = SCALE * 1.4426950408889634
HIDDEN = -1e30
F32 = jnp.float32
BF16 = jnp.bfloat16


def dot(a, b, dim_a, dim_b):
    return lax.dot_general(a, b, (((dim_a,), (dim_b,)), ((), ())), preferred_element_type=F32)


def make_kernel(devices, inner, rows, chunk):
    halo = SPAN * rows
    span = halo + rows
    band = halo + chunk

    def kernel(
        q_hbm, k_hbm, v_hbm, g_hbm, b_hbm,
        dq_hbm, dk_hbm, dv_hbm,
        q_in, g_in, k_in, v_in, b_in, dq_out, q16, g16, kv, hide, acc, wide, dq32,
        to_near, to_other, near_in, other_in, far_out, far_in, own_out, own_in,
        in_sem, out_sem, kv_send, kv_recv, pair_send, pair_recv, back_send, back_recv,
    ):
        me = lax.axis_index("outer") * inner + lax.axis_index("inner")
        odd = lax.rem(me, 2)
        even = odd == 0
        partner = me + 1 - 2 * odd

        def at(index):
            return (index // inner, lax.rem(index, inner))

        has_before = me >= 2
        has_after = me + 2 < devices
        far_before = me >= SPAN
        far_after = me + SPAN < devices

        barrier = pltpu.get_barrier_semaphore()
        for step, there in ((2, has_before), (SPAN, far_before)):

            @pl.when(there)
            def _():
                pl.semaphore_signal(
                    barrier, inc=1, device_id=at(me - step), device_id_type=MESH
                )

        @pl.when(odd == 1)
        def _():
            pl.semaphore_signal(barrier, inc=1, device_id=at(partner), device_id_type=MESH)

        copies = [
            pltpu.make_async_copy(source, target, in_sem.at[i])
            for i, (source, target) in enumerate(
                ((k_hbm, k_in), (v_hbm, v_in), (b_hbm, b_in), (q_hbm, q_in), (g_hbm, g_in))
            )
        ]
        for copy in copies:
            copy.start()

        for part, ref in ((0, k_in), (1, v_in)):
            copies[part].wait()
            wide[part] = ref[...].astype(F32)
            for c in range(KVH):
                own = wide[part, pl.ds(c, rows, stride=KVH), :]
                kv[c, part, pl.ds(halo, rows), :] = own.astype(BF16)

        waits = (1 - odd) + has_after.astype(jnp.int32) + far_after.astype(jnp.int32)

        @pl.when(waits > 0)
        def _():
            pl.semaphore_wait(barrier, waits)

        def block(c, offset):
            start = (SPAN - offset) * rows
            if not isinstance(start, int):
                start = pl.multiple_of(start, rows)
            return kv.at[c, :, pl.ds(start, rows), :]

        def ahead(c, offset):
            return pltpu.make_async_remote_copy(
                block(c, 0), block(c, offset), kv_send.at[offset // 2 - 1, c],
                kv_recv.at[offset // 2 - 1, c], device_id=at(me + offset), device_id_type=MESH,
            )

        def across(c, offset):
            kind = 2 + offset // 2
            return pltpu.make_async_remote_copy(
                block(c, offset - 1 + 2 * odd), block(c, offset), kv_send.at[kind, c],
                kv_recv.at[kind, c], device_id=at(partner), device_id_type=MESH,
            )

        def own_ahead(c):
            @pl.when(has_after)
            def _():
                ahead(c, 2).start()

            @pl.when(far_after)
            def _():
                ahead(c, SPAN).start()

        def next_ahead(c):
            @pl.when(has_after)
            def _():
                ahead(c - 1, 2).wait_send()

            @pl.when(far_after)
            def _():
                ahead(c - 1, SPAN).wait_send()

            own_ahead(c)

        def relay(c):
            @pl.when(odd == 1)
            def _():
                across(c, 1).wait_recv()

            @pl.when(has_before)
            def _():
                ahead(c, 2).wait_recv()

                @pl.when(even)
                def _():
                    across(c, 3).start()

                @pl.when(odd == 1)
                def _():
                    across(c, 1).start()

        def relay_far(c):
            @pl.when(far_before)
            def _():
                ahead(c, SPAN).wait_recv()

                @pl.when(odd == 1)
                def _():
                    across(c, 3).start()

        def all_here(c):
            @pl.when(even & has_before)
            def _():
                across(c, 1).wait_recv()

            @pl.when(far_before | (me == 3))
            def _():
                across(c, 3).wait_recv()

        own_ahead(0)

        @pl.when(even)
        def _():
            for c in range(KVH):
                across(c, 1).start()

        for offset in range(1, SPAN + 1):

            @pl.when(me < offset)
            def _():
                for c in range(KVH):
                    kv[c, :, pl.ds((SPAN - offset) * rows, rows), :] = jnp.zeros(
                        (2, rows, HD), BF16
                    )

        @pl.when(jnp.logical_not(has_after))
        def _():
            own_in[...] = jnp.zeros(own_in.shape, BF16)

        @pl.when(jnp.logical_not(far_after))
        def _():
            far_in[...] = jnp.zeros(far_in.shape, BF16)

        copies[2].wait()
        b_ref = b_in
        base = (me - SPAN) * rows
        pos = lax.broadcasted_iota(jnp.int32, (span, rows), 0) + base
        query = lax.broadcasted_iota(jnp.int32, (span, rows), 1) + (base + halo)
        seen = (
            (pos >= b_ref[0:1, :])
            & (pos <= query)
            & ((pos < b_ref[1:2, :]) | (pos >= b_ref[2:3, :]))
        )
        hide[...] = jnp.where(seen, 0.0, HIDDEN).astype(BF16)

        def arrange(copy, source, target):
            copy.wait()
            for half in range(QH // 16):
                x = source[:, pl.ds(16 * half, 16), :].astype(F32)
                for k in range(16 // GROUP):
                    y = x[:, GROUP * k : GROUP * (k + 1), :].reshape(rows * GROUP, HD)
                    target[half * (16 // GROUP) + k] = y.astype(BF16)

        arrange(copies[3], q_in, q16)
        next_ahead(1)
        arrange(copies[4], g_in, g16)

        def compute(c, j):
            many = chunk * GROUP
            first = j * chunk
            key = kv[c, 0, pl.ds(first, band), :]
            value = kv[c, 1, pl.ds(first, band), :]
            queries = q16[c, pl.ds(first * GROUP, many), :]
            grads = g16[c, pl.ds(first * GROUP, many), :]
            lane = lax.broadcasted_iota(jnp.int32, (many, rows), 1)
            token = lax.broadcasted_iota(jnp.int32, (many, rows), 0) // GROUP + first
            mine = (lane == token).astype(BF16)
            scores = dot(
                jnp.concatenate([key, hide[pl.ds(first, band), :]], axis=1),
                jnp.concatenate([queries, mine], axis=1),
                1, 1,
            )
            grad_weights = dot(value, grads, 1, 1)
            top = jnp.max(scores, axis=0, keepdims=True)
            raw = jnp.exp2(scores * SCALE2 - top * SCALE2)
            total = jnp.sum(raw, axis=0, keepdims=True)
            weighted = jnp.sum(raw * grad_weights, axis=0, keepdims=True)
            inverse = 1.0 / total
            prob = raw * inverse
            dscore = (prob * (grad_weights - weighted * inverse)).astype(BF16)
            weights = prob.astype(BF16)
            for part, left, right in ((0, dscore, queries), (1, weights, grads)):
                add = dot(left, right, 1, 0)
                if j == 0:
                    acc[c, part, pl.ds(0, band), :] = add
                    acc[c, part, pl.ds(band, span - band), :] = jnp.zeros((span - band, HD), F32)
                else:
                    acc[c, part, pl.ds(first, band), :] += add
            query_part = dot(dscore, key, 0, 0) * SCALE
            dq32[pl.ds(first, chunk), pl.ds(GROUP * c, GROUP), :] = query_part.reshape(
                chunk, GROUP, HD
            )

        def pair(c, kind, source, target):
            return pltpu.make_async_remote_copy(
                source.at[c], target.at[c], pair_send.at[kind, c], pair_recv.at[kind, c],
                device_id=at(partner), device_id_type=MESH,
            )

        def back(c, kind, source, target):
            return pltpu.make_async_remote_copy(
                source.at[c], target.at[c], back_send.at[kind, c], back_recv.at[kind, c],
                device_id=at(me - 2 - 2 * kind), device_id_type=MESH,
            )

        odd_f = odd.astype(F32)

        def send_pair(c):
            near = pl.multiple_of(halo - rows - 2 * rows * odd, rows)
            other = pl.multiple_of(rows + 2 * rows * odd, rows)
            to_other[c] = acc[c, :, pl.ds(other, rows), :].astype(BF16)
            pair(c, 0, to_other, other_in).start()
            to_near[c] = acc[c, :, pl.ds(near, rows), :].astype(BF16)
            pair(c, 1, to_near, near_in).start()

        def send_back(c):
            pair(c, 0, to_other, other_in).wait_recv()
            far = acc[c, :, pl.ds(0, rows), :] + odd_f * other_in[c].astype(F32)
            far_out[c] = far.astype(BF16)

            @pl.when(far_before)
            def _():
                back(c, 1, far_out, far_in).start()

            pair(c, 1, to_near, near_in).wait_recv()
            near = acc[c, :, pl.ds(2 * rows, rows), :] + near_in[c].astype(F32)
            own_out[c] = near.astype(BF16)

            @pl.when(has_before)
            def _():
                back(c, 0, own_out, own_in).start()

        def finish(c):
            own = acc[c, :, pl.ds(halo, rows), :] + (1.0 - odd_f) * other_in[c].astype(F32)

            @pl.when(has_after)
            def _():
                back(c, 0, own_out, own_in).wait_recv()

            @pl.when(far_after)
            def _():
                back(c, 1, far_out, far_in).wait_recv()

            own = own + own_in[c].astype(F32) + far_in[c].astype(F32)
            wide[0, pl.ds(c, rows, stride=KVH), :] = own[0] * SCALE
            wide[1, pl.ds(c, rows, stride=KVH), :] = own[1]

        relay(0)
        relay_far(0)
        next_ahead(2)
        all_here(0)
        for c in range(KVH):
            if c > 0:
                all_here(c)
            for j in range(rows // chunk):
                compute(c, j)
                if j == 0:
                    if c == 0:
                        next_ahead(3)
                    if c + 1 < KVH:
                        relay(c + 1)
                    if c >= 1:
                        send_back(c - 1)
                    if c + 1 < KVH:
                        relay_far(c + 1)
            send_pair(c)
            if c % 2 == 1:
                pick = pl.ds(GROUP * (c - 1), 2 * GROUP)
                dq_out[:, pick, :] = dq32[:, pick, :].astype(BF16)
                copy = pltpu.make_async_copy(
                    dq_out.at[:, pick, :], dq_hbm.at[:, pick, :], out_sem.at[c // 2]
                )
                copy.start()
                copies.append(copy)
        finish(0)
        send_back(KVH - 1)
        finish(1)
        finish(2)
        finish(3)
        for part, (source, target) in enumerate(((k_in, dk_hbm), (v_in, dv_hbm))):
            source[...] = wide[part].astype(BF16)
            copy = pltpu.make_async_copy(source, target, out_sem.at[2 + part])
            copy.start()
            copies.append(copy)
        for copy in copies[5:]:
            copy.wait()

        for c in range(KVH):
            pair(c, 0, to_other, other_in).wait_send()
            pair(c, 1, to_near, near_in).wait_send()

            @pl.when(has_before)
            def _():
                back(c, 0, own_out, own_in).wait_send()

            @pl.when(far_before)
            def _():
                back(c, 1, far_out, far_in).wait_send()

            if c == KVH - 1:

                @pl.when(has_after)
                def _():
                    ahead(c, 2).wait_send()

                @pl.when(far_after)
                def _():
                    ahead(c, SPAN).wait_send()

            @pl.when(even | has_before)
            def _():
                across(c, 1).wait_send()

            @pl.when((even & has_before) | far_before)
            def _():
                across(c, 3).wait_send()

    return kernel


def write_out(*refs):
    sources, targets, spaces, (sems,) = refs[:3], refs[3:6], refs[6:9], refs[9:]
    pieces = []
    for source, target, space in zip(sources, targets, spaces):
        cuts = 4 if len(source.shape) == 3 else 1
        size = source.shape[0] // cuts
        for i in range(cuts):
            pick = pl.ds(i * size, size)
            n = len(pieces)
            pieces.append(
                (
                    pltpu.make_async_copy(source.at[pick], space.at[pick], sems.at[0, n]),
                    pltpu.make_async_copy(space.at[pick], target.at[pick], sems.at[1, n]),
                )
            )
    for inward, _ in pieces:
        inward.start()
    for inward, outward in pieces:
        inward.wait()
        outward.start()
    for _, outward in pieces:
        outward.wait()


def solution(mesh):
    outer, inner = mesh.shape["outer"], mesh.shape["inner"]
    devices = outer * inner

    def per_device(queries, key_states, value_states, out_grad, bounds):
        rows = queries.shape[0]
        chunk = min(64, rows // 2)
        span = (SPAN + 1) * rows
        piece = pltpu.VMEM((KVH, 2, rows, HD), BF16)
        hbm = pl.BlockSpec(memory_space=pltpu.HBM)
        flat = (rows * KVH, HD)
        query_grad, key_grad, value_grad = pl.pallas_call(
            make_kernel(devices, inner, rows, chunk),
            out_shape=[
                jax.ShapeDtypeStruct((rows, QH, HD), BF16),
                jax.ShapeDtypeStruct(flat, BF16),
                jax.ShapeDtypeStruct(flat, BF16),
            ],
            in_specs=[hbm] * 5,
            out_specs=[hbm] * 3,
            scratch_shapes=[
                pltpu.VMEM((rows, QH, HD), BF16),
                pltpu.VMEM((rows, QH, HD), BF16),
                pltpu.VMEM(flat, BF16),
                pltpu.VMEM(flat, BF16),
                pltpu.VMEM(bounds.shape, jnp.int32),
                pltpu.VMEM((rows, QH, HD), BF16),
                pltpu.VMEM((KVH, rows * GROUP, HD), BF16),
                pltpu.VMEM((KVH, rows * GROUP, HD), BF16),
                pltpu.VMEM((KVH, 2, span, HD), BF16),
                pltpu.VMEM((span, rows), BF16),
                pltpu.VMEM((KVH, 2, span, HD), F32),
                pltpu.VMEM((2, rows * KVH, HD), F32),
                pltpu.VMEM((rows, QH, HD), F32),
                piece, piece, piece, piece, piece, piece, piece, piece,
                pltpu.SemaphoreType.DMA((5,)),
                pltpu.SemaphoreType.DMA((4,)),
                pltpu.SemaphoreType.DMA((4, KVH)),
                pltpu.SemaphoreType.DMA((4, KVH)),
                pltpu.SemaphoreType.DMA((2, KVH)),
                pltpu.SemaphoreType.DMA((2, KVH)),
                pltpu.SemaphoreType.DMA((2, KVH)),
                pltpu.SemaphoreType.DMA((2, KVH)),
            ],
            compiler_params=pltpu.CompilerParams(
                collective_id=0, has_side_effects=True, vmem_limit_bytes=56 * 2**20
            ),
            cost_estimate=pl.CostEstimate(
                flops=10 * QH * rows * span * HD,
                bytes_accessed=8 * rows * (QH + KVH) * HD,
                transcendentals=QH * rows * span,
            ),
        )(
            queries, key_states.reshape(flat), value_states.reshape(flat), out_grad, bounds
        )
        grads = (query_grad, key_grad, value_grad)
        query_grad, key_grad, value_grad = pl.pallas_call(
            write_out,
            out_shape=[jax.ShapeDtypeStruct(x.shape, x.dtype) for x in grads],
            in_specs=[hbm] * 3,
            out_specs=[hbm] * 3,
            scratch_shapes=[pltpu.VMEM(x.shape, x.dtype) for x in grads]
            + [pltpu.SemaphoreType.DMA((2, 6))],
            compiler_params=pltpu.CompilerParams(vmem_limit_bytes=56 * 2**20),
        )(*grads)
        back = key_states.shape
        return query_grad, key_grad.reshape(back), value_grad.reshape(back)

    split = ("outer", "inner")
    whole = P(split, None, None)
    return jax.shard_map(
        per_device,
        mesh=mesh,
        in_specs=(whole, whole, whole, whole, P(None, split)),
        out_specs=(whole, whole, whole),
        check_vma=False,
    )
```

```python
import jax
import jax.numpy as jnp
from jax import lax
from jax.experimental import pallas as pl
from jax.experimental.pallas import tpu as pltpu
from jax.sharding import PartitionSpec as P

QH = 32
KVH = 4
HD = 128
SPAN = 4
GROUP = QH // KVH
MESH = pl.DeviceIdType.MESH
SCALE = HD**-0.5
SCALE2 = SCALE * 1.4426950408889634
HIDDEN = -1e30
F32 = jnp.float32
BF16 = jnp.bfloat16


def dot(a, b, dim_a, dim_b):
    return lax.dot_general(a, b, (((dim_a,), (dim_b,)), ((), ())), preferred_element_type=F32)


def make_kernel(devices, inner, rows, chunk):
    halo = SPAN * rows
    span = halo + rows
    band = halo + chunk

    def kernel(
        q_hbm, k_hbm, v_hbm, g_hbm, b_hbm,
        dq_hbm, dk_hbm, dv_hbm,
        q_in, g_in, k_in, v_in, b_in, dq_out, q16, g16, kv, hide, acc, wide, dq32,
        to_near, to_other, near_in, other_in, far_out, far_in, own_out, own_in,
        in_sem, out_sem, kv_send, kv_recv, pair_send, pair_recv, back_send, back_recv,
    ):
        me = lax.axis_index("outer") * inner + lax.axis_index("inner")
        odd = lax.rem(me, 2)
        even = odd == 0
        partner = me + 1 - 2 * odd

        def at(index):
            return (index // inner, lax.rem(index, inner))

        has_before = me >= 2
        has_after = me + 2 < devices
        far_before = me >= SPAN
        far_after = me + SPAN < devices

        barrier = pltpu.get_barrier_semaphore()
        for step, there in ((2, has_before), (SPAN, far_before)):

            @pl.when(there)
            def _():
                pl.semaphore_signal(
                    barrier, inc=1, device_id=at(me - step), device_id_type=MESH
                )

        @pl.when(odd == 1)
        def _():
            pl.semaphore_signal(barrier, inc=1, device_id=at(partner), device_id_type=MESH)

        copies = [
            pltpu.make_async_copy(source, target, in_sem.at[i])
            for i, (source, target) in enumerate(
                ((k_hbm, k_in), (v_hbm, v_in), (b_hbm, b_in), (q_hbm, q_in), (g_hbm, g_in))
            )
        ]
        for copy in copies:
            copy.start()

        for part, ref in ((0, k_in), (1, v_in)):
            copies[part].wait()
            wide[part] = ref[...].astype(F32)
            for c in range(KVH):
                own = wide[part, pl.ds(c, rows, stride=KVH), :]
                kv[c, part, pl.ds(halo, rows), :] = own.astype(BF16)

        waits = (1 - odd) + has_after.astype(jnp.int32) + far_after.astype(jnp.int32)

        @pl.when(waits > 0)
        def _():
            pl.semaphore_wait(barrier, waits)

        def block(c, offset):
            start = (SPAN - offset) * rows
            if not isinstance(start, int):
                start = pl.multiple_of(start, rows)
            return kv.at[c, :, pl.ds(start, rows), :]

        def ahead(c, offset):
            return pltpu.make_async_remote_copy(
                block(c, 0), block(c, offset), kv_send.at[offset // 2 - 1, c],
                kv_recv.at[offset // 2 - 1, c], device_id=at(me + offset), device_id_type=MESH,
            )

        def across(c, offset):
            kind = 2 + offset // 2
            return pltpu.make_async_remote_copy(
                block(c, offset - 1 + 2 * odd), block(c, offset), kv_send.at[kind, c],
                kv_recv.at[kind, c], device_id=at(partner), device_id_type=MESH,
            )

        def own_ahead(c):
            @pl.when(has_after)
            def _():
                ahead(c, 2).start()

            @pl.when(far_after)
            def _():
                ahead(c, SPAN).start()

        def next_ahead(c):
            @pl.when(has_after)
            def _():
                ahead(c - 1, 2).wait_send()

            @pl.when(far_after)
            def _():
                ahead(c - 1, SPAN).wait_send()

            own_ahead(c)

        def relay(c):
            @pl.when(odd == 1)
            def _():
                across(c, 1).wait_recv()

            @pl.when(has_before)
            def _():
                ahead(c, 2).wait_recv()

                @pl.when(even)
                def _():
                    across(c, 3).start()

                @pl.when(odd == 1)
                def _():
                    across(c, 1).start()

        def relay_far(c):
            @pl.when(far_before)
            def _():
                ahead(c, SPAN).wait_recv()

                @pl.when(odd == 1)
                def _():
                    across(c, 3).start()

        def all_here(c):
            @pl.when(even & has_before)
            def _():
                across(c, 1).wait_recv()

            @pl.when(far_before | (me == 3))
            def _():
                across(c, 3).wait_recv()

        own_ahead(0)

        @pl.when(even)
        def _():
            for c in range(KVH):
                across(c, 1).start()

        for offset in range(1, SPAN + 1):

            @pl.when(me < offset)
            def _():
                for c in range(KVH):
                    kv[c, :, pl.ds((SPAN - offset) * rows, rows), :] = jnp.zeros(
                        (2, rows, HD), BF16
                    )

        @pl.when(jnp.logical_not(has_after))
        def _():
            own_in[...] = jnp.zeros(own_in.shape, BF16)

        @pl.when(jnp.logical_not(far_after))
        def _():
            far_in[...] = jnp.zeros(far_in.shape, BF16)

        copies[2].wait()
        b_ref = b_in
        base = (me - SPAN) * rows
        pos = lax.broadcasted_iota(jnp.int32, (span, rows), 0) + base
        query = lax.broadcasted_iota(jnp.int32, (span, rows), 1) + (base + halo)
        seen = (
            (pos >= b_ref[0:1, :])
            & (pos <= query)
            & ((pos < b_ref[1:2, :]) | (pos >= b_ref[2:3, :]))
        )
        hide[...] = jnp.where(seen, 0.0, HIDDEN).astype(BF16)

        def arrange(copy, source, target):
            copy.wait()
            for half in range(QH // 16):
                x = source[:, pl.ds(16 * half, 16), :].astype(F32)
                for k in range(16 // GROUP):
                    y = x[:, GROUP * k : GROUP * (k + 1), :].reshape(rows * GROUP, HD)
                    target[half * (16 // GROUP) + k] = y.astype(BF16)

        arrange(copies[3], q_in, q16)
        next_ahead(1)
        arrange(copies[4], g_in, g16)

        def compute(c, j):
            many = chunk * GROUP
            first = j * chunk
            key = kv[c, 0, pl.ds(first, band), :]
            value = kv[c, 1, pl.ds(first, band), :]
            queries = q16[c, pl.ds(first * GROUP, many), :]
            grads = g16[c, pl.ds(first * GROUP, many), :]
            lane = lax.broadcasted_iota(jnp.int32, (many, rows), 1)
            token = lax.broadcasted_iota(jnp.int32, (many, rows), 0) // GROUP + first
            mine = (lane == token).astype(BF16)
            scores = dot(
                jnp.concatenate([key, hide[pl.ds(first, band), :]], axis=1),
                jnp.concatenate([queries, mine], axis=1),
                1, 1,
            )
            grad_weights = dot(value, grads, 1, 1)
            top = jnp.max(scores, axis=0, keepdims=True)
            raw = jnp.exp2(scores * SCALE2 - top * SCALE2)
            total = jnp.sum(raw, axis=0, keepdims=True)
            weighted = jnp.sum(raw * grad_weights, axis=0, keepdims=True)
            inverse = 1.0 / total
            prob = raw * inverse
            dscore = (prob * (grad_weights - weighted * inverse)).astype(BF16)
            weights = prob.astype(BF16)
            for part, left, right in ((0, dscore, queries), (1, weights, grads)):
                add = dot(left, right, 1, 0)
                if j == 0:
                    acc[c, part, pl.ds(0, band), :] = add
                    acc[c, part, pl.ds(band, span - band), :] = jnp.zeros((span - band, HD), F32)
                else:
                    acc[c, part, pl.ds(first, band), :] += add
            query_part = dot(dscore, key, 0, 0) * SCALE
            dq32[pl.ds(first, chunk), pl.ds(GROUP * c, GROUP), :] = query_part.reshape(
                chunk, GROUP, HD
            )

        def pair(c, kind, source, target):
            return pltpu.make_async_remote_copy(
                source.at[c], target.at[c], pair_send.at[kind, c], pair_recv.at[kind, c],
                device_id=at(partner), device_id_type=MESH,
            )

        def back(c, kind, source, target):
            return pltpu.make_async_remote_copy(
                source.at[c], target.at[c], back_send.at[kind, c], back_recv.at[kind, c],
                device_id=at(me - 2 - 2 * kind), device_id_type=MESH,
            )

        odd_f = odd.astype(F32)

        def send_pair(c):
            near = pl.multiple_of(halo - rows - 2 * rows * odd, rows)
            other = pl.multiple_of(rows + 2 * rows * odd, rows)
            to_near[c] = acc[c, :, pl.ds(near, rows), :].astype(BF16)
            pair(c, 1, to_near, near_in).start()
            to_other[c] = acc[c, :, pl.ds(other, rows), :].astype(BF16)
            pair(c, 0, to_other, other_in).start()

        def send_back(c):
            pair(c, 1, to_near, near_in).wait_recv()
            near = acc[c, :, pl.ds(2 * rows, rows), :] + near_in[c].astype(F32)
            own_out[c] = near.astype(BF16)

            @pl.when(has_before)
            def _():
                back(c, 0, own_out, own_in).start()

            pair(c, 0, to_other, other_in).wait_recv()
            far = acc[c, :, pl.ds(0, rows), :] + odd_f * other_in[c].astype(F32)
            far_out[c] = far.astype(BF16)

            @pl.when(far_before)
            def _():
                back(c, 1, far_out, far_in).start()

        def finish(c):
            own = acc[c, :, pl.ds(halo, rows), :] + (1.0 - odd_f) * other_in[c].astype(F32)

            @pl.when(has_after)
            def _():
                back(c, 0, own_out, own_in).wait_recv()

            @pl.when(far_after)
            def _():
                back(c, 1, far_out, far_in).wait_recv()

            own = own + own_in[c].astype(F32) + far_in[c].astype(F32)
            wide[0, pl.ds(c, rows, stride=KVH), :] = own[0] * SCALE
            wide[1, pl.ds(c, rows, stride=KVH), :] = own[1]

        next_ahead(2)
        relay(0)
        relay_far(0)
        next_ahead(3)
        for c in range(KVH):
            all_here(c)
            if c >= 1:
                send_back(c - 1)
            for j in range(rows // chunk):
                compute(c, j)
            send_pair(c)
            if c + 1 < KVH:
                relay(c + 1)
                relay_far(c + 1)
            if c % 2 == 1:
                pick = pl.ds(GROUP * (c - 1), 2 * GROUP)
                dq_out[:, pick, :] = dq32[:, pick, :].astype(BF16)
                copy = pltpu.make_async_copy(
                    dq_out.at[:, pick, :], dq_hbm.at[:, pick, :], out_sem.at[c // 2]
                )
                copy.start()
                copies.append(copy)
        finish(0)
        send_back(KVH - 1)
        finish(1)
        finish(2)
        finish(3)
        for part, (source, target) in enumerate(((k_in, dk_hbm), (v_in, dv_hbm))):
            source[...] = wide[part].astype(BF16)
            copy = pltpu.make_async_copy(source, target, out_sem.at[2 + part])
            copy.start()
            copies.append(copy)
        for copy in copies[5:]:
            copy.wait()

        for c in range(KVH):
            pair(c, 0, to_other, other_in).wait_send()
            pair(c, 1, to_near, near_in).wait_send()

            @pl.when(has_before)
            def _():
                back(c, 0, own_out, own_in).wait_send()

            @pl.when(far_before)
            def _():
                back(c, 1, far_out, far_in).wait_send()

            if c == KVH - 1:

                @pl.when(has_after)
                def _():
                    ahead(c, 2).wait_send()

                @pl.when(far_after)
                def _():
                    ahead(c, SPAN).wait_send()

            @pl.when(even | has_before)
            def _():
                across(c, 1).wait_send()

            @pl.when((even & has_before) | far_before)
            def _():
                across(c, 3).wait_send()

    return kernel


def write_out(*refs):
    sources, targets, spaces, (sems,) = refs[:3], refs[3:6], refs[6:9], refs[9:]
    pieces = []
    for source, target, space in zip(sources, targets, spaces):
        cuts = 4 if len(source.shape) == 3 else 1
        size = source.shape[0] // cuts
        for i in range(cuts):
            pick = pl.ds(i * size, size)
            n = len(pieces)
            pieces.append(
                (
                    pltpu.make_async_copy(source.at[pick], space.at[pick], sems.at[0, n]),
                    pltpu.make_async_copy(space.at[pick], target.at[pick], sems.at[1, n]),
                )
            )
    for inward, _ in pieces:
        inward.start()
    for inward, outward in pieces:
        inward.wait()
        outward.start()
    for _, outward in pieces:
        outward.wait()


def solution(mesh):
    outer, inner = mesh.shape["outer"], mesh.shape["inner"]
    devices = outer * inner

    def per_device(queries, key_states, value_states, out_grad, bounds):
        rows = queries.shape[0]
        chunk = min(64, rows // 2)
        span = (SPAN + 1) * rows
        piece = pltpu.VMEM((KVH, 2, rows, HD), BF16)
        hbm = pl.BlockSpec(memory_space=pltpu.HBM)
        flat = (rows * KVH, HD)
        query_grad, key_grad, value_grad = pl.pallas_call(
            make_kernel(devices, inner, rows, chunk),
            out_shape=[
                jax.ShapeDtypeStruct((rows, QH, HD), BF16),
                jax.ShapeDtypeStruct(flat, BF16),
                jax.ShapeDtypeStruct(flat, BF16),
            ],
            in_specs=[hbm] * 5,
            out_specs=[hbm] * 3,
            scratch_shapes=[
                pltpu.VMEM((rows, QH, HD), BF16),
                pltpu.VMEM((rows, QH, HD), BF16),
                pltpu.VMEM(flat, BF16),
                pltpu.VMEM(flat, BF16),
                pltpu.VMEM(bounds.shape, jnp.int32),
                pltpu.VMEM((rows, QH, HD), BF16),
                pltpu.VMEM((KVH, rows * GROUP, HD), BF16),
                pltpu.VMEM((KVH, rows * GROUP, HD), BF16),
                pltpu.VMEM((KVH, 2, span, HD), BF16),
                pltpu.VMEM((span, rows), BF16),
                pltpu.VMEM((KVH, 2, span, HD), F32),
                pltpu.VMEM((2, rows * KVH, HD), F32),
                pltpu.VMEM((rows, QH, HD), F32),
                piece, piece, piece, piece, piece, piece, piece, piece,
                pltpu.SemaphoreType.DMA((5,)),
                pltpu.SemaphoreType.DMA((4,)),
                pltpu.SemaphoreType.DMA((4, KVH)),
                pltpu.SemaphoreType.DMA((4, KVH)),
                pltpu.SemaphoreType.DMA((2, KVH)),
                pltpu.SemaphoreType.DMA((2, KVH)),
                pltpu.SemaphoreType.DMA((2, KVH)),
                pltpu.SemaphoreType.DMA((2, KVH)),
            ],
            compiler_params=pltpu.CompilerParams(
                collective_id=0, has_side_effects=True, vmem_limit_bytes=56 * 2**20
            ),
            cost_estimate=pl.CostEstimate(
                flops=10 * QH * rows * span * HD,
                bytes_accessed=8 * rows * (QH + KVH) * HD,
                transcendentals=QH * rows * span,
            ),
        )(
            queries, key_states.reshape(flat), value_states.reshape(flat), out_grad, bounds
        )
        grads = (query_grad, key_grad, value_grad)
        query_grad, key_grad, value_grad = pl.pallas_call(
            write_out,
            out_shape=[jax.ShapeDtypeStruct(x.shape, x.dtype) for x in grads],
            in_specs=[hbm] * 3,
            out_specs=[hbm] * 3,
            scratch_shapes=[pltpu.VMEM(x.shape, x.dtype) for x in grads]
            + [pltpu.SemaphoreType.DMA((2, 6))],
            compiler_params=pltpu.CompilerParams(vmem_limit_bytes=56 * 2**20),
        )(*grads)
        back = key_states.shape
        return query_grad, key_grad.reshape(back), value_grad.reshape(back)

    split = ("outer", "inner")
    whole = P(split, None, None)
    return jax.shard_map(
        per_device,
        mesh=mesh,
        in_specs=(whole, whole, whole, whole, P(None, split)),
        out_specs=(whole, whole, whole),
        check_vma=False,
    )
```
